128 devices in a mesh: ctx: 32 (over z, y, core), head: 4 (over x).
Axes of the slice: x: 4, y: 4, z: 4, core: 2. Of those that a mesh axis runs over, the one named last changes fastest.
Arguments:
- ctx_query: bfloat16 [32768, 4096], P('ctx', 'head'), may hold values from -30 to 30
- ctx_key: bfloat16 [32768, 1024], P('ctx', 'head'), may hold values from -13.5625 to 13.5625
- ctx_value: bfloat16 [32768, 1024], P('ctx', 'head'), may hold values from -6 to 6
- quest_query: bfloat16 [256, 4096], P(None, 'head'), may hold values from -30 to 30
- quest_key: bfloat16 [256, 1024], P(None, 'head'), may hold values from -13.5625 to 13.5625
- quest_value: bfloat16 [256, 1024], P(None, 'head'), may hold values from -6 to 6
- quest_order: int32 [256], replicated, may hold values from 0 to 255, each once
- out_weight: bfloat16 [4096, 4096], P('head'), may hold values from -0.09375 to 0.09375
Outputs:
- ctx_out: bfloat16 [32768, 4096], P('ctx', 'head')
- answer: bfloat16 [256, 4096], P('ctx', 'head')
The draws below stay inside these ranges and needn't reach their ends.
Inputs may be any that keep to these rules, and one draw needn't show every extreme that they name: `quest_order`: each of 0 to 255 appears once.
All inputs are finite; a program needn't handle non-finite values.
Results may differ from the reference program's by a relative error of at most 0.005.
Values may be sent and summed in bfloat16 or wider, within the bound.
No kernel may reach another device: no remote copies, remote signals or barrier semaphores. Data moves between devices by JAX's collectives and lax.ppermute only.
A program may use at most 256 MiB of HBM per device.

```python
import math
import jax
import jax.numpy as jnp
from jax import lax

D = 4096
HEADS = 32
KV_HEADS = 8
HEAD_DIM = 128
BLOCK = 1024
QROWS = 256
TOKENS = 32768
N_CTX = 32


def normal_rows(key, row_count, col_count, base_scale):
    values = jax.random.truncated_normal(key, -8.0, 8.0, (row_count, col_count), jnp.float32)
    return (values * base_scale).astype(jnp.bfloat16)


def draw_ctx_query(key, part):
    key = jax.random.fold_in(key, 11)
    return normal_rows(key, TOKENS, HEADS * HEAD_DIM, 1.7)


def draw_quest_query(key, part):
    key = jax.random.fold_in(key, 23)
    return normal_rows(key, QROWS, HEADS * HEAD_DIM, 1.7)


def steps_of(own_key, shape, shards, smallest, largest):
    gain, own = 1.0, jax.random.fold_in(own_key, 6)
    for axis_at, blocks in shards:
        steps = jnp.exp(jax.random.uniform(jax.random.fold_in(own, axis_at), (blocks,), jnp.float32, smallest / len(shards), largest / len(shards)))
        gain = gain * jnp.repeat(steps, shape[axis_at] // blocks).reshape([-1 if axis == axis_at else 1 for axis in range(len(shape))])
    return gain


def bell_draw(rng, dims, scale, bound, cuts=(), held_as=jnp.bfloat16):
    result = jax.random.normal(rng, dims, jnp.float32) * scale
    if len(cuts) > 0:
        result = steps_of(rng, dims, cuts, -0.22, 0.18) * result
    return jnp.clip(result, min=-bound, max=bound).astype(held_as)


def setup_inputs(seed: int = 0) -> dict:
    splits = jax.random.split(jax.random.key(seed), 9)
    return {
        "ctx_query": draw_ctx_query(jax.random.fold_in(splits[8], 71), 0),
        "ctx_key": bell_draw(splits[1], (TOKENS, KV_HEADS * HEAD_DIM), 1.7, 13.5625, ((0, 32), (1, 4))),
        "ctx_value": bell_draw(splits[2], (TOKENS, KV_HEADS * HEAD_DIM), 1.0, 6.0, ((0, 32), (1, 4))),
        "quest_query": draw_quest_query(jax.random.fold_in(splits[8], 71), 0),
        "quest_key": bell_draw(splits[4], (QROWS, KV_HEADS * HEAD_DIM), 1.7, 13.5625, ((1, 4),)),
        "quest_value": bell_draw(splits[5], (QROWS, KV_HEADS * HEAD_DIM), 1.0, 6.0, ((1, 4),)),
        "quest_order": jax.random.permutation(splits[6], QROWS).astype(jnp.int32),
        "out_weight": bell_draw(splits[7], (HEADS * HEAD_DIM, D), (HEADS * HEAD_DIM) ** -0.5, 0.09375, ((0, 4),)),
    }


def attend_block(queries, cached_keys, cached_values, allowed):
    row_count = queries.shape[0]
    kv_count = cached_keys.shape[1] // HEAD_DIM
    group_size = queries.shape[1] // cached_keys.shape[1]
    query_heads = queries.reshape(row_count, kv_count, group_size, HEAD_DIM).astype(jnp.float32)
    key_heads = cached_keys.reshape(-1, kv_count, HEAD_DIM).astype(jnp.float32)
    value_heads = cached_values.reshape(-1, kv_count, HEAD_DIM).astype(jnp.float32)
    scores = jnp.einsum('rkgd,ckd->kgrc', query_heads, key_heads) / math.sqrt(HEAD_DIM)
    scores = jnp.where(allowed, scores, -jnp.inf)
    maxima = lax.optimization_barrier(jnp.max(scores, axis=-1))
    weights = jnp.exp(scores - maxima[..., None])
    totals = lax.optimization_barrier(jnp.sum(weights, axis=-1))
    rounded = weights.astype(jnp.bfloat16).astype(jnp.float32)
    weighted = jnp.einsum('kgrc,ckd->rkgd', rounded, value_heads)
    return (jnp.transpose(maxima, (2, 0, 1)).reshape(row_count, -1), jnp.transpose(totals, (2, 0, 1)).reshape(row_count, -1), weighted.reshape(row_count, -1))

def reference(ctx_query, ctx_key, ctx_value, quest_query, quest_key, quest_value, quest_order, out_weight):
    anchor_keys = ctx_key[:BLOCK]
    anchor_values = ctx_value[:BLOCK]
    row_ids = lax.broadcasted_iota(jnp.int32, (BLOCK, BLOCK), 0)
    col_ids = lax.broadcasted_iota(jnp.int32, (BLOCK, BLOCK), 1)
    causal = col_ids <= row_ids

    def context_block(block_index):
        first_row = (block_index * BLOCK).astype(jnp.int32)
        queries = lax.dynamic_slice_in_dim(ctx_query, first_row, BLOCK, 0)
        own_keys = lax.dynamic_slice_in_dim(ctx_key, first_row, BLOCK, 0)
        own_values = lax.dynamic_slice_in_dim(ctx_value, first_row, BLOCK, 0)
        all_keys = jnp.concatenate([anchor_keys, own_keys], axis=0)
        all_values = jnp.concatenate([anchor_values, own_values], axis=0)
        allowed = jnp.concatenate([jnp.broadcast_to(block_index > 0, (BLOCK, BLOCK)), causal], axis=1)
        maxima, totals, weighted = attend_block(queries, all_keys, all_values, allowed)
        return (weighted / jnp.repeat(totals, HEAD_DIM, axis=1)).astype(jnp.bfloat16)
    block_ids = jnp.arange(N_CTX, dtype=jnp.int32)
    ctx_out = lax.map(context_block, block_ids).reshape(TOKENS, HEADS * HEAD_DIM)

    def question_block(block_index):
        first_row = (block_index * BLOCK).astype(jnp.int32)
        own_keys = lax.dynamic_slice_in_dim(ctx_key, first_row, BLOCK, 0)
        own_values = lax.dynamic_slice_in_dim(ctx_value, first_row, BLOCK, 0)
        return attend_block(quest_query, own_keys, own_values, True)
    block_max, block_total, block_sum = lax.map(question_block, block_ids)
    order_allowed = quest_order[None, :] <= quest_order[:, None]
    self_max, self_total, self_sum = attend_block(quest_query, quest_key, quest_value, order_allowed)
    peak = jnp.maximum(lax.optimization_barrier(jnp.max(block_max, axis=0)), self_max)
    block_scale = jnp.exp(block_max - peak[None])
    self_scale = jnp.exp(self_max - peak)
    totals = lax.optimization_barrier(jnp.sum(block_total * block_scale, axis=0)) + self_total * self_scale
    combined = lax.optimization_barrier(jnp.sum(block_sum * jnp.repeat(block_scale, HEAD_DIM, axis=2), axis=0))
    combined = combined + self_sum * jnp.repeat(self_scale, HEAD_DIM, axis=1)
    attended = (combined / jnp.repeat(totals, HEAD_DIM, axis=1)).astype(jnp.bfloat16)
    answer = jnp.dot(attended, out_weight, preferred_element_type=jnp.float32).astype(jnp.bfloat16)
    return (ctx_out, answer)
```

```python
import math

import jax
import jax.numpy as jnp
from jax import lax
from jax.experimental import pallas as pl
from jax.experimental.pallas import tpu as pltpu
from jax.sharding import PartitionSpec as P

HEAD_DIM = 128
BLOCK = 1024
TILE = 256
QROWS = 256
GROUP = 4
HEADS = 8
EXTRA = 128
SCALE = math.log2(math.e) / math.sqrt(HEAD_DIM)
F32 = jnp.float32
BF16 = jnp.bfloat16
VMEM_LIMIT = 48 * 1024 * 1024


def scores_of(queries, keys):
    return lax.dot_general(queries, keys, (((1,), (1,)), ((), ())), preferred_element_type=F32)


def weigh(scores):
    maxima = jnp.max(scores, axis=-1, keepdims=True)
    weights = jnp.exp2((scores - maxima) * SCALE)
    return maxima, weights, jnp.sum(weights, axis=-1, keepdims=True)


def times_values(weights, values):
    return jnp.dot(weights.astype(BF16), values, preferred_element_type=F32)


def head_cols(head):
    return slice(head * HEAD_DIM, (head + 1) * HEAD_DIM)


def question_kernel(query_ref, key_ref, value_ref, out_ref, lse_ref):
    lse_ref[...] = jnp.zeros_like(lse_ref)
    for head in range(HEADS):
        kv = head // GROUP
        scores = scores_of(query_ref[:, head_cols(head)], key_ref[:, head_cols(kv)])
        maxima, weights, totals = weigh(scores)
        summed = times_values(weights, value_ref[:, head_cols(kv)])
        out_ref[:, head_cols(head)] = (summed / totals).astype(BF16)
        rest = maxima * SCALE + jnp.log2(totals)
        for part in range(3):
            term = rest.astype(BF16).astype(F32)
            at = part * HEADS + head
            lse_ref[:, at : at + 1] = term
            rest = rest - term
    out_ref[:, HEADS * HEAD_DIM :] = lse_ref[...].astype(BF16)


def question_part(quest_query, ctx_key, ctx_value):
    rows, width = quest_query.shape
    return pl.pallas_call(
        question_kernel,
        out_shape=jax.ShapeDtypeStruct((rows, width + EXTRA), BF16),
        scratch_shapes=[pltpu.VMEM((rows, EXTRA), F32)],
        compiler_params=pltpu.CompilerParams(vmem_limit_bytes=VMEM_LIMIT),
        cost_estimate=pl.CostEstimate(
            flops=4 * rows * width * BLOCK, bytes_accessed=2 << 20, transcendentals=rows * HEADS * BLOCK
        ),
        name="question_block",
    )(quest_query, ctx_key, ctx_value)


def self_kernel(place_ref, order_ref, query_ref, key_ref, value_ref, order_row_ref, out_ref, lse_ref):
    first = (place_ref[0] // 2) * 16
    row_ids = lax.broadcasted_iota(jnp.int32, (16, QROWS), 0)
    row_order = jnp.zeros((16, QROWS), jnp.int32)
    for row in range(16):
        row_order = jnp.where(row_ids == row, order_ref[first + row], row_order)
    allowed = order_row_ref[...] <= row_order
    upper = place_ref[0] % 2 == 1
    lane = lax.broadcasted_iota(jnp.int32, (8, EXTRA), 1)
    lse = jnp.zeros((8, EXTRA), F32)
    for head in range(HEADS):
        kv = head // GROUP
        scores = scores_of(query_ref[:, head_cols(head)], key_ref[:, head_cols(kv)])
        scores = jnp.where(allowed, scores, -jnp.inf)
        maxima, weights, totals = weigh(scores)
        summed = times_values(weights, value_ref[:, head_cols(kv)]) / totals
        row_lse = maxima * SCALE + jnp.log2(totals)
        out_ref[:, head_cols(head)] = jnp.where(upper, summed[8:], summed[:8])
        lse = jnp.where(lane == head, jnp.where(upper, row_lse[8:], row_lse[:8]), lse)
    lse_ref[...] = lse


def self_part(place, quest_query, quest_key, quest_value, quest_order):
    width = quest_query.shape[1]
    kv_width = quest_key.shape[1]
    whole = lambda i, place, order: (0, 0)
    return pl.pallas_call(
        self_kernel,
        out_shape=(
            jax.ShapeDtypeStruct((8, width), F32),
            jax.ShapeDtypeStruct((8, EXTRA), F32),
        ),
        grid_spec=pltpu.PrefetchScalarGridSpec(
            num_scalar_prefetch=2,
            grid=(1,),
            in_specs=[
                pl.BlockSpec((16, width), lambda i, place, order: (place[0] // 2, 0)),
                pl.BlockSpec((QROWS, kv_width), whole),
                pl.BlockSpec((QROWS, kv_width), whole),
                pl.BlockSpec((1, QROWS), whole),
            ],
            out_specs=(pl.BlockSpec((8, width), whole), pl.BlockSpec((8, EXTRA), whole)),
        ),
        cost_estimate=pl.CostEstimate(flops=1 << 28, bytes_accessed=1 << 19, transcendentals=1 << 15),
        name="question_self",
    )(place, quest_order, quest_query, quest_key, quest_value, quest_order.reshape(1, QROWS))


def combine_kernel(parts_ref, self_ref, self_lse_ref, weight_ref, out_ref, attended_ref):
    @pl.when(pl.program_id(0) == 0)
    def _():
        blocks = parts_ref.shape[0] // 8
        width = HEADS * HEAD_DIM
        terms = parts_ref[:, width:].astype(F32)
        lse = terms + pltpu.roll(terms, EXTRA - HEADS, 1) + pltpu.roll(terms, EXTRA - 2 * HEADS, 1)
        lse = lse.reshape(blocks, 8, EXTRA)
        peak = jnp.maximum(jnp.max(lse, axis=0), self_lse_ref[...])
        scale = jnp.exp2(lse - peak[None])
        self_scale = jnp.exp2(self_lse_ref[...] - peak)
        inverse = 1.0 / (jnp.sum(scale, axis=0) + self_scale)
        scale = scale * inverse[None]
        self_scale = self_scale * inverse
        for head in range(HEADS):
            total = self_ref[:, head_cols(head)] * self_scale[:, head : head + 1]
            part = parts_ref[:, head_cols(head)].astype(F32).reshape(blocks, 8, HEAD_DIM)
            total = total + jnp.sum(part * scale[:, :, head : head + 1], axis=0)
            attended_ref[:, head_cols(head)] = total

    out_ref[0] = jnp.dot(
        attended_ref[...].astype(BF16), weight_ref[...], preferred_element_type=F32
    )


def combine_part(parts, self_out, self_lse, out_weight):
    depth, columns = out_weight.shape
    step = columns // 4
    whole = lambda i: (0, 0)
    return pl.pallas_call(
        combine_kernel,
        out_shape=jax.ShapeDtypeStruct((4, 8, step), F32),
        grid=(4,),
        in_specs=[
            pl.BlockSpec(parts.shape, whole),
            pl.BlockSpec(self_out.shape, whole),
            pl.BlockSpec(self_lse.shape, whole),
            pl.BlockSpec((depth, step), lambda i: (0, i)),
        ],
        out_specs=pl.BlockSpec((1, 8, step), lambda i: (i, 0, 0)),
        scratch_shapes=[pltpu.VMEM((8, depth), F32)],
        compiler_params=pltpu.CompilerParams(vmem_limit_bytes=VMEM_LIMIT),
        cost_estimate=pl.CostEstimate(flops=2 * 8 * depth * columns, bytes_accessed=9 << 20, transcendentals=0),
        name="question_merge",
    )(parts, self_out, self_lse, out_weight)


def local_kernel(query_ref, key_ref, value_ref, sum_ref, stat_ref):
    kv, tile = pl.program_id(0), pl.program_id(1)
    row_ids = lax.broadcasted_iota(jnp.int32, (TILE, TILE), 0)
    col_ids = lax.broadcasted_iota(jnp.int32, (TILE, TILE), 1)
    causal = col_ids <= row_ids
    for at in range(BLOCK // TILE):

        @pl.when(tile == at)
        def _(at=at):
            before = at * TILE
            for head in range(GROUP):
                queries = query_ref[:, head_cols(head)]
                scores = scores_of(queries, key_ref[: before + TILE, :])
                last = jnp.where(causal, scores[:, before:], -jnp.inf)
                if before:
                    scores = jnp.concatenate([scores[:, :before], last], axis=1)
                else:
                    scores = last
                maxima, weights, totals = weigh(scores)
                sum_ref[:, head_cols(head)] = times_values(weights, value_ref[: before + TILE, :])
                stat_ref[0, :, head : head + 1] = maxima
                stat_ref[0, :, GROUP + head : GROUP + head + 1] = totals


def local_part(ctx_query, ctx_key, ctx_value):
    rows, width = ctx_query.shape
    group = GROUP * HEAD_DIM
    return pl.pallas_call(
        local_kernel,
        out_shape=(
            jax.ShapeDtypeStruct((rows, width), F32),
            jax.ShapeDtypeStruct((2, rows, EXTRA), F32),
        ),
        grid=(2, rows // TILE),
        in_specs=[
            pl.BlockSpec((TILE, group), lambda kv, tile: (tile, kv)),
            pl.BlockSpec((rows, HEAD_DIM), lambda kv, tile: (0, kv)),
            pl.BlockSpec((rows, HEAD_DIM), lambda kv, tile: (0, kv)),
        ],
        out_specs=(
            pl.BlockSpec((TILE, group), lambda kv, tile: (tile, kv)),
            pl.BlockSpec((1, TILE, EXTRA), lambda kv, tile: (kv, tile, 0)),
        ),
        compiler_params=pltpu.CompilerParams(vmem_limit_bytes=VMEM_LIMIT),
        cost_estimate=pl.CostEstimate(
            flops=4 * rows * width * BLOCK, bytes_accessed=8 << 20, transcendentals=rows * HEADS * BLOCK // 2
        ),
        name="context_own",
    )(ctx_query, ctx_key, ctx_value)


def anchor_kernel(place_ref, query_ref, key_ref, value_ref, sum_ref, stat_ref, *rest):
    out_ref = rest[-1]
    is_anchor = place_ref[1] == 0
    for head in range(GROUP):
        scores = scores_of(query_ref[:, head_cols(head)], key_ref[...])
        maxima, weights, totals = weigh(scores)
        summed = times_values(weights, value_ref[...])
        own_max = stat_ref[0, :, head : head + 1]
        own_total = stat_ref[0, :, GROUP + head : GROUP + head + 1]
        maxima = jnp.where(is_anchor, -jnp.inf, maxima)
        peak = jnp.maximum(maxima, own_max)
        scale = jnp.exp2((maxima - peak) * SCALE)
        own_scale = jnp.exp2((own_max - peak) * SCALE)
        inverse = 1.0 / (totals * scale + own_total * own_scale)
        out_ref[:, head_cols(head)] = (
            summed * (scale * inverse) + sum_ref[:, head_cols(head)] * (own_scale * inverse)
        ).astype(BF16)


def anchor_part(place, ctx_query, keys, values, own_sum, own_stat, so_far):
    rows, width = ctx_query.shape
    group = GROUP * HEAD_DIM
    tile_of = lambda tile, place: (tile, place[0])
    whole = lambda tile, place: (0, 0)
    operands = [ctx_query, keys, values, own_sum, own_stat]
    in_specs = [
        pl.BlockSpec((TILE, group), tile_of),
        pl.BlockSpec((rows, HEAD_DIM), whole),
        pl.BlockSpec((rows, HEAD_DIM), whole),
        pl.BlockSpec((TILE, group), tile_of),
        pl.BlockSpec((1, TILE, EXTRA), lambda tile, place: (place[0], tile, 0)),
    ]
    aliases = {}
    if so_far is not None:
        operands.append(so_far)
        in_specs.append(pl.BlockSpec(memory_space=pl.ANY))
        aliases = {6: 0}
    return pl.pallas_call(
        anchor_kernel,
        out_shape=jax.ShapeDtypeStruct((rows, width), BF16),
        grid_spec=pltpu.PrefetchScalarGridSpec(
            num_scalar_prefetch=1,
            grid=(rows // TILE,),
            in_specs=in_specs,
            out_specs=pl.BlockSpec((TILE, group), tile_of),
        ),
        input_output_aliases=aliases,
        compiler_params=pltpu.CompilerParams(vmem_limit_bytes=VMEM_LIMIT),
        cost_estimate=pl.CostEstimate(
            flops=2 * rows * width * BLOCK, bytes_accessed=6 << 20, transcendentals=rows * GROUP * BLOCK
        ),
        name="context_anchor",
    )(place, *operands)


def device_at(z, y, core):
    return (z * 4 + y) * 2 + core


def edges(phase, steps):
    pairs = []
    for core in range(2):
        for first, last in steps:
            for other in range(1 if phase == 0 else 4):
                along_y = (core == 0) == (phase == 0)
                ends = [
                    device_at(other, at, core) if along_y else device_at(at, other, core)
                    for at in (first, last)
                ]
                pairs.append(tuple(ends))
    return pairs


SIBLINGS = [(at, at ^ 1) for at in range(32)]


def per_device(
    ctx_query, ctx_key, ctx_value, quest_query, quest_key, quest_value, quest_order, out_weight
):
    me = lax.axis_index("ctx")
    core = lax.rem(me, 2)
    first_half = jnp.concatenate([ctx_key[:, :HEAD_DIM], ctx_value[:, :HEAD_DIM]], axis=0)
    second_half = jnp.concatenate([ctx_key[:, HEAD_DIM:], ctx_value[:, HEAD_DIM:]], axis=0)
    moved = lax.ppermute(second_half, "ctx", [(0, 1)])
    half = jnp.where(me == 0, first_half, moved)
    for phase in range(2):
        half = half + lax.ppermute(half, "ctx", edges(phase, [(0, 1)]))
        half = half + lax.ppermute(half, "ctx", edges(phase, [(0, 3), (1, 2)]))
    other_half = lax.ppermute(half, "ctx", SIBLINGS)

    parts = question_part(quest_query, ctx_key, ctx_value)
    parts = lax.all_to_all(
        parts.reshape(32, 8, parts.shape[1]), "ctx", split_axis=0, concat_axis=0, tiled=True
    ).reshape(parts.shape)
    place = jnp.stack([me, me]).astype(jnp.int32)
    self_out, self_lse = self_part(place, quest_query, quest_key, quest_value, quest_order)
    own_sum, own_stat = local_part(ctx_query, ctx_key, ctx_value)
    projected = combine_part(parts, self_out, self_lse, out_weight)
    projected = lax.all_to_all(projected, "head", split_axis=0, concat_axis=0, tiled=True)
    answer = jnp.sum(projected, axis=0).astype(BF16)
    here = jnp.stack([core, me]).astype(jnp.int32)
    there = jnp.stack([1 - core, me]).astype(jnp.int32)
    ctx_out = anchor_part(here, ctx_query, half[:BLOCK], half[BLOCK:], own_sum, own_stat, None)
    ctx_out = anchor_part(
        there, ctx_query, other_half[:BLOCK], other_half[BLOCK:], own_sum, own_stat, ctx_out
    )
    return (ctx_out, answer)


def solution(mesh):
    in_specs = (
        P("ctx", "head"),
        P("ctx", "head"),
        P("ctx", "head"),
        P(None, "head"),
        P(None, "head"),
        P(None, "head"),
        P(),
        P("head", None),
    )
    out_specs = (P("ctx", "head"), P("ctx", "head"))
    return jax.shard_map(
        per_device, mesh=mesh, in_specs=in_specs, out_specs=out_specs, check_vma=False
    )
```

```python
import math

import jax
import jax.numpy as jnp
from jax import lax
from jax.experimental import pallas as pl
from jax.experimental.pallas import tpu as pltpu
from jax.sharding import PartitionSpec as P

HEAD_DIM = 128
BLOCK = 1024
TILE = 256
QROWS = 256
GROUP = 4
HEADS = 8
EXTRA = 128
SCALE = math.log2(math.e) / math.sqrt(HEAD_DIM)
F32 = jnp.float32
BF16 = jnp.bfloat16
VMEM_LIMIT = 56 * 1024 * 1024
ANCHOR_ROWS = 512


def scores_of(queries, keys):
    return lax.dot_general(queries, keys, (((1,), (1,)), ((), ())), preferred_element_type=F32)


def weigh(scores):
    maxima = jnp.max(scores, axis=-1, keepdims=True)
    weights = jnp.exp2((scores - maxima) * SCALE)
    return maxima, weights, jnp.sum(weights, axis=-1, keepdims=True)


def whole(*shape):
    return pl.BlockSpec(shape, lambda step: (0,) * len(shape))


def columns_of(rows, width, at):
    return pl.BlockSpec((rows, width), lambda step: (0, at))


SCALARS = pl.BlockSpec(memory_space=pltpu.SMEM)
IN_HBM = pl.BlockSpec(memory_space=pltpu.HBM)


def times_values(weights, values):
    return jnp.dot(weights.astype(BF16), values, preferred_element_type=F32)


def head_cols(head):
    return slice(head * HEAD_DIM, (head + 1) * HEAD_DIM)


def staggered(items, scores_at, finish):
    scores = scores_at(items[0])
    for at, item in enumerate(items):
        later = scores_at(items[at + 1]) if at + 1 < len(items) else None
        finish(item, scores)
        scores = later


class Local:
    SCRATCH = [
        pltpu.VMEM((BLOCK, GROUP * HEAD_DIM), BF16),
        pltpu.VMEM((BLOCK, HEAD_DIM), BF16),
        pltpu.VMEM((BLOCK, HEAD_DIM), BF16),
        pltpu.VMEM((BLOCK, GROUP * HEAD_DIM), F32),
        pltpu.VMEM((BLOCK, EXTRA), F32),
        pltpu.SemaphoreType.DMA((BLOCK // TILE,)),
        pltpu.SemaphoreType.DMA((2 * (BLOCK // TILE),)),
        pltpu.SemaphoreType.DMA((2 * (BLOCK // TILE),)),
    ]

    def __init__(self, kv, hbm, scratch):
        self.query_hbm, self.key_hbm, self.value_hbm, self.sum_out, self.stat_out = hbm
        self.query_ref, self.key_ref, self.value_ref, self.sum_ref, self.stat_ref = scratch[:5]
        query_sems, kv_sems, self.sems = scratch[5:]
        query_cols = pl.ds(pl.multiple_of(kv * GROUP * HEAD_DIM, HEAD_DIM), GROUP * HEAD_DIM)
        kv_cols = pl.ds(pl.multiple_of(kv * HEAD_DIM, HEAD_DIM), HEAD_DIM)
        self.loads = []
        for tile in range(BLOCK // TILE):
            rows = pl.ds(tile * TILE, TILE)
            self.loads.append(
                [
                    pltpu.make_async_copy(
                        self.key_hbm.at[rows, kv_cols], self.key_ref.at[rows], kv_sems.at[2 * tile]
                    ),
                    pltpu.make_async_copy(
                        self.query_hbm.at[rows, query_cols], self.query_ref.at[rows], query_sems.at[tile]
                    ),
                    pltpu.make_async_copy(
                        self.value_hbm.at[rows, kv_cols], self.value_ref.at[rows], kv_sems.at[2 * tile + 1]
                    ),
                ]
            )

    def load(self):
        for tile in self.loads:
            for copy in tile:
                copy.start()

    def run(self):
        row_ids = lax.broadcasted_iota(jnp.int32, (TILE, TILE), 0)
        col_ids = lax.broadcasted_iota(jnp.int32, (TILE, TILE), 1)
        causal = col_ids <= row_ids
        lane = lax.broadcasted_iota(jnp.int32, (TILE, EXTRA), 1)
        stats, copies = {}, []

        def send(source, target, rows):
            copy = pltpu.make_async_copy(source.at[rows], target.at[rows], self.sems.at[len(copies)])
            copy.start()
            copies.append(copy)

        def scores_at(item):
            tile, head = item
            if head == 0:
                for copy in self.loads[tile]:
                    copy.wait()
            rows = slice(tile * TILE, (tile + 1) * TILE)
            return scores_of(self.query_ref[rows, head_cols(head)], self.key_ref[: (tile + 1) * TILE, :])

        def finish(item, scores):
            tile, head = item
            rows = slice(tile * TILE, (tile + 1) * TILE)
            before = tile * TILE
            last = jnp.where(causal, scores[:, before:], -jnp.inf)
            scores = jnp.concatenate([scores[:, :before], last], axis=1) if before else last
            maxima, weights, totals = weigh(scores)
            values = self.value_ref[: before + TILE, :]
            self.sum_ref[rows, head_cols(head)] = times_values(weights, values)
            stat = stats.get(tile, jnp.zeros((TILE, EXTRA), F32))
            stat = jnp.where(lane == head, maxima, stat)
            stats[tile] = jnp.where(lane == GROUP + head, totals, stat)
            if head == GROUP - 1:
                self.stat_ref[rows, :] = stats[tile]
                send(self.sum_ref, self.sum_out, rows)
                send(self.stat_ref, self.stat_out, rows)

        tiles = range(BLOCK // TILE)
        staggered([(tile, head) for tile in tiles for head in range(GROUP)], scores_at, finish)
        for copy in copies:
            copy.wait()


def local_kernel(place_ref, *refs):
    local = Local(place_ref[0], refs[:5], refs[5:])
    local.load()
    local.run()


LOCAL_OUT = (
    jax.ShapeDtypeStruct((BLOCK, GROUP * HEAD_DIM), F32),
    jax.ShapeDtypeStruct((BLOCK, EXTRA), F32),
)


def local_part(place, ctx_query, ctx_key, ctx_value):
    return pl.pallas_call(
        local_kernel,
        out_shape=LOCAL_OUT,
        grid=(1,),
        in_specs=[SCALARS] + [IN_HBM] * 3,
        out_specs=(IN_HBM,) * 2,
        scratch_shapes=Local.SCRATCH,
        compiler_params=pltpu.CompilerParams(vmem_limit_bytes=VMEM_LIMIT),
        cost_estimate=pl.CostEstimate(flops=1 << 26, bytes_accessed=1 << 18, transcendentals=1 << 16),
        name="context_own",
    )(place, ctx_query, ctx_key, ctx_value)


def question_kernel(
    place_ref,
    order_ref,
    query_ref,
    key_ref,
    value_ref,
    self_key_ref,
    self_value_ref,
    order_row_ref,
    ctx_query_hbm,
    ctx_key_hbm,
    ctx_value_hbm,
    out_ref,
    self_ref,
    self_lse_ref,
    sum_out,
    stat_out,
    *scratch,
):
    own = Local(
        place_ref[0] % 2, (ctx_query_hbm, ctx_key_hbm, ctx_value_hbm, sum_out, stat_out), scratch
    )
    own.load()
    lane = lax.broadcasted_iota(jnp.int32, (QROWS, EXTRA), 1)
    packed = [jnp.zeros((QROWS, EXTRA), F32)]
    first = pl.multiple_of((place_ref[0] // 2) * 16, 16)
    upper = place_ref[0] % 2 == 1
    row_ids = lax.broadcasted_iota(jnp.int32, (16, QROWS), 0)
    row_order = jnp.zeros((16, QROWS), jnp.int32)
    for row in range(16):
        row_order = jnp.where(row_ids == row, order_ref[first + row], row_order)
    allowed = jnp.concatenate([order_row_ref[...] <= row_order] * GROUP, axis=0)
    lse = jnp.zeros((8, EXTRA), F32)

    def scores_at(head):
        return scores_of(query_ref[:, head_cols(head)], key_ref[:, head_cols(head // GROUP)])

    def finish(head, scores):
        maxima, weights, totals = weigh(scores)
        summed = times_values(weights, value_ref[:, head_cols(head // GROUP)])
        out_ref[:, head_cols(head)] = (summed / totals).astype(BF16)
        packed[0] = jnp.where(lane == head, maxima * SCALE + jnp.log2(totals), packed[0])

    staggered(range(HEADS), scores_at, finish)
    rest, terms = packed[0], None
    for part in range(3):
        term = rest.astype(BF16).astype(F32)
        rest = rest - term
        terms = term if part == 0 else terms + pltpu.roll(term, part * HEADS, 1)
    out_ref[:, HEADS * HEAD_DIM :] = terms.astype(BF16)

    for kv in range(HEADS // GROUP):
        heads = range(kv * GROUP, (kv + 1) * GROUP)
        queries = jnp.concatenate(
            [query_ref[pl.ds(first, 16), head_cols(head)] for head in heads], axis=0
        )
        scores = scores_of(queries, self_key_ref[:, head_cols(kv)])
        maxima, weights, totals = weigh(jnp.where(allowed, scores, -jnp.inf))
        summed = times_values(weights, self_value_ref[:, head_cols(kv)]) / totals
        row_lse = maxima * SCALE + jnp.log2(totals)
        for at, head in enumerate(heads):
            low, high = slice(at * 16, at * 16 + 8), slice(at * 16 + 8, at * 16 + 16)
            self_ref[:, head_cols(head)] = jnp.where(upper, summed[high], summed[low])
            lse = jnp.where(lane[:8] == head, jnp.where(upper, row_lse[high], row_lse[low]), lse)
    self_lse_ref[...] = lse
    own.run()


def question_part(
    place, quest_query, ctx_query, ctx_key, ctx_value, quest_key, quest_value, quest_order
):
    rows, width = quest_query.shape
    return pl.pallas_call(
        question_kernel,
        out_shape=(
            jax.ShapeDtypeStruct((rows, width + EXTRA), BF16),
            jax.ShapeDtypeStruct((8, width), F32),
            jax.ShapeDtypeStruct((8, EXTRA), F32),
            *LOCAL_OUT,
        ),
        grid=(1,),
        in_specs=[
            SCALARS,
            SCALARS,
            whole(rows, width),
            whole(*ctx_key.shape),
            whole(*ctx_value.shape),
            whole(*quest_key.shape),
            whole(*quest_value.shape),
            whole(1, QROWS),
            IN_HBM,
            IN_HBM,
            IN_HBM,
        ],
        out_specs=(
            whole(rows, width + EXTRA),
            whole(8, width),
            whole(8, EXTRA),
            IN_HBM,
            IN_HBM,
        ),
        scratch_shapes=Local.SCRATCH,
        compiler_params=pltpu.CompilerParams(vmem_limit_bytes=VMEM_LIMIT),
        cost_estimate=pl.CostEstimate(flops=1 << 26, bytes_accessed=1 << 18, transcendentals=1 << 16),
        name="question_block",
    )(
        place,
        quest_order,
        quest_query,
        ctx_key,
        ctx_value,
        quest_key,
        quest_value,
        quest_order.reshape(1, QROWS),
        ctx_query,
        ctx_key,
        ctx_value,
    )


def combine_kernel(
    parts_hbm, self_ref, self_lse_ref, weight_hbm, out_ref, parts_ref, weight_ref, sems
):
    step = out_ref.shape[2]
    arrived = pltpu.make_async_copy(parts_hbm, parts_ref, sems.at[4])
    arrived.start()
    loads = []
    for at in range(out_ref.shape[0]):
        cols = pl.ds(at * step, step)
        loads.append(
            pltpu.make_async_copy(weight_hbm.at[:, cols], weight_ref.at[:, cols], sems.at[at])
        )
        loads[-1].start()
    arrived.wait()
    blocks = parts_ref.shape[0] // 8
    width = HEADS * HEAD_DIM
    terms = parts_ref[:, width:].astype(F32)
    lse = terms + pltpu.roll(terms, EXTRA - HEADS, 1) + pltpu.roll(terms, EXTRA - 2 * HEADS, 1)
    lse = lse.reshape(blocks, 8, EXTRA)
    peak = jnp.maximum(jnp.max(lse, axis=0), self_lse_ref[...])
    scale = jnp.exp2(lse - peak[None])
    self_scale = jnp.exp2(self_lse_ref[...] - peak)
    inverse = 1.0 / (jnp.sum(scale, axis=0) + self_scale)
    scale = scale * inverse[None]
    self_scale = self_scale * inverse
    attended = []
    for head in range(HEADS):
        total = self_ref[:, head_cols(head)] * self_scale[:, head : head + 1]
        part = parts_ref[:, head_cols(head)].astype(F32).reshape(blocks, 8, HEAD_DIM)
        attended.append(total + jnp.sum(part * scale[:, :, head : head + 1], axis=0))
    attended = jnp.concatenate(attended, axis=1).astype(BF16)
    for at, load in enumerate(loads):
        load.wait()
        out_ref[at] = jnp.dot(
            attended, weight_ref[:, at * step : (at + 1) * step], preferred_element_type=F32
        )


def combine_part(parts, self_out, self_lse, out_weight):
    depth, columns = out_weight.shape
    return pl.pallas_call(
        combine_kernel,
        out_shape=jax.ShapeDtypeStruct((4, 8, columns // 4), F32),
        grid=(1,),
        in_specs=[
            IN_HBM,
            whole(*self_out.shape),
            whole(*self_lse.shape),
            IN_HBM,
        ],
        out_specs=whole(4, 8, columns // 4),
        scratch_shapes=[
            pltpu.VMEM(parts.shape, BF16),
            pltpu.VMEM((depth, columns), BF16),
            pltpu.SemaphoreType.DMA((5,)),
        ],
        compiler_params=pltpu.CompilerParams(vmem_limit_bytes=VMEM_LIMIT),
        cost_estimate=pl.CostEstimate(flops=2 * 8 * depth * columns, bytes_accessed=9 << 20, transcendentals=0),
        name="question_merge",
    )(parts, self_out, self_lse, out_weight)


def anchor_kernel(place_ref, query_ref, key_ref, value_ref, sum_ref, stat_ref, *rest):
    out_ref, summed_ref = rest[-2:]
    is_anchor = place_ref[1] == 0
    lane = lax.broadcasted_iota(jnp.int32, (TILE, EXTRA), 1)
    packed = {}

    def scores_at(item):
        row, head = item
        return scores_of(query_ref[row : row + TILE, head_cols(head)], key_ref[...])

    def finish(item, scores):
        row, head = item
        rows = slice(row, row + TILE)
        maxima, weights, totals = weigh(scores)
        summed_ref[rows, head_cols(head)] = times_values(weights, value_ref[...])
        all_maxima, all_totals = packed.get(row, (jnp.zeros((TILE, EXTRA), F32),) * 2)
        all_maxima = jnp.where(lane == head, maxima, all_maxima)
        all_totals = jnp.where(lane == head, totals, all_totals)
        packed[row] = all_maxima, all_totals
        if head == GROUP - 1:
            merge(rows, all_maxima, all_totals)

    def merge(rows, maxima, totals):
        own_max = stat_ref[rows, :]
        own_total = pltpu.roll(own_max, EXTRA - GROUP, 1)
        maxima = jnp.where(is_anchor, -jnp.inf, maxima)
        peak = jnp.maximum(maxima, own_max)
        scale = jnp.exp2((maxima - peak) * SCALE)
        own_scale = jnp.exp2((own_max - peak) * SCALE)
        inverse = 1.0 / (totals * scale + own_total * own_scale)
        scale, own_scale = scale * inverse, own_scale * inverse
        for head in range(GROUP):
            cols = head_cols(head)
            out_ref[rows, cols] = (
                summed_ref[rows, cols] * scale[:, head : head + 1]
                + sum_ref[rows, cols] * own_scale[:, head : head + 1]
            ).astype(BF16)

    rows = range(0, ANCHOR_ROWS, TILE)
    staggered([(row, head) for row in rows for head in range(GROUP)], scores_at, finish)


def anchor_part(place, ctx_query, half, own_sum, own_stat, so_far):
    rows, width = ctx_query.shape
    group = GROUP * HEAD_DIM
    tile_of = lambda tile, place: (tile, place[0])
    row_of = lambda tile, place: (tile, 0)
    operands = [ctx_query, half, half, own_sum, own_stat]
    in_specs = [
        pl.BlockSpec((ANCHOR_ROWS, group), tile_of),
        pl.BlockSpec((BLOCK, HEAD_DIM), lambda tile, place: (0, 0)),
        pl.BlockSpec((BLOCK, HEAD_DIM), lambda tile, place: (0, 1)),
        pl.BlockSpec((ANCHOR_ROWS, group), row_of),
        pl.BlockSpec((ANCHOR_ROWS, EXTRA), row_of),
    ]
    aliases = {}
    if so_far is not None:
        operands.append(so_far)
        in_specs.append(pl.BlockSpec(memory_space=pl.ANY))
        aliases = {6: 0}
    return pl.pallas_call(
        anchor_kernel,
        out_shape=jax.ShapeDtypeStruct((rows, width), BF16),
        grid_spec=pltpu.PrefetchScalarGridSpec(
            num_scalar_prefetch=1,
            grid=(rows // ANCHOR_ROWS,),
            in_specs=in_specs,
            out_specs=pl.BlockSpec((ANCHOR_ROWS, group), tile_of),
            scratch_shapes=[pltpu.VMEM((ANCHOR_ROWS, group), F32)],
        ),
        input_output_aliases=aliases,
        compiler_params=pltpu.CompilerParams(vmem_limit_bytes=VMEM_LIMIT),
        cost_estimate=pl.CostEstimate(
            flops=1 << 26, bytes_accessed=1 << 18, transcendentals=1 << 16
        ),
        name="context_anchor",
    )(place, *operands)


def after(value, *others):
    return lax.optimization_barrier((value, *others))[0]


def exchange(value, axis, groups=None):
    return lax.all_to_all(
        value, axis, split_axis=0, concat_axis=0, axis_index_groups=groups, tiled=True
    )


def per_device(
    ctx_query, ctx_key, ctx_value, quest_query, quest_key, quest_value, quest_order, out_weight
):
    me = lax.axis_index("ctx").astype(jnp.int32)
    devices = lax.axis_size("ctx")
    core = lax.rem(me, 2)
    place = me.reshape(1)
    here, there = jnp.stack([core, me]), jnp.stack([1 - core, me])
    groups = [list(range(at, devices, 2)) for at in range(2)]
    siblings = [(at, at ^ 1) for at in range(devices)]
    first, second = slice(0, HEAD_DIM), slice(HEAD_DIM, 2 * HEAD_DIM)

    keys = lax.ppermute(ctx_key, "ctx", [(0, 1)])
    values = lax.ppermute(ctx_value, "ctx", [(0, 1)])
    half = jnp.where(
        me == 0,
        jnp.concatenate([ctx_key[:, first], ctx_value[:, first]], axis=1),
        jnp.concatenate([keys[:, second], values[:, second]], axis=1),
    )
    chips = devices // 2
    shares = exchange(half.reshape(chips, BLOCK // chips, 2 * HEAD_DIM), "ctx", groups)[0]

    parts, self_out, self_lse, *own_here = question_part(
        place, quest_query, ctx_query, ctx_key, ctx_value, quest_key, quest_value, quest_order
    )
    shares = after(shares, self_lse)
    half = exchange(jnp.broadcast_to(shares[None], (chips, *shares.shape)), "ctx", groups)
    own_there = local_part(after(there, shares), ctx_query, ctx_key, ctx_value)
    half = after(half.reshape(BLOCK, 2 * HEAD_DIM), own_there[1])
    other_half = lax.ppermute(half, "ctx", siblings)

    width = parts.shape[1]
    parts = exchange(after(parts, half).reshape(devices, -1, width), "ctx").reshape(QROWS, width)
    ctx_out = anchor_part(here, ctx_query, half, *own_here, None)
    parts = after(parts, ctx_out)
    projected = combine_part(parts, self_out, self_lse, out_weight)
    there = after(there, projected)
    projected = exchange(projected, "head")
    ctx_out = anchor_part(there, ctx_query, other_half, *own_there, ctx_out)
    answer = jnp.sum(after(projected, ctx_out), axis=0).astype(BF16)
    return (ctx_out, answer)


def solution(mesh):
    in_specs = (
        P("ctx", "head"),
        P("ctx", "head"),
        P("ctx", "head"),
        P(None, "head"),
        P(None, "head"),
        P(None, "head"),
        P(),
        P("head", None),
    )
    out_specs = (P("ctx", "head"), P("ctx", "head"))
    return jax.shard_map(
        per_device, mesh=mesh, in_specs=in_specs, out_specs=out_specs, check_vma=False
    )
```

```python
import math

import jax
import jax.numpy as jnp
from jax import lax
from jax.experimental import pallas as pl
from jax.experimental.pallas import tpu as pltpu
from jax.sharding import PartitionSpec as P

HEAD_DIM = 128
BLOCK = 1024
TILE = 256
QROWS = 256
GROUP = 4
HEADS = 8
EXTRA = 128
SCALE = math.log2(math.e) / math.sqrt(HEAD_DIM)
F32 = jnp.float32
BF16 = jnp.bfloat16
VMEM_LIMIT = 56 * 1024 * 1024
ANCHOR_ROWS = 512


def scores_of(queries, keys):
    return lax.dot_general(queries, keys, (((1,), (1,)), ((), ())), preferred_element_type=F32)


def weigh(scores):
    maxima = jnp.max(scores, axis=-1, keepdims=True)
    weights = jnp.exp2((scores - maxima) * SCALE)
    return maxima, weights, jnp.sum(weights, axis=-1, keepdims=True)


def whole(*shape):
    return pl.BlockSpec(shape, lambda step: (0,) * len(shape))


def columns_of(rows, width, at):
    return pl.BlockSpec((rows, width), lambda step: (0, at))


SCALARS = pl.BlockSpec(memory_space=pltpu.SMEM)


def times_values(weights, values):
    return jnp.dot(weights.astype(BF16), values, preferred_element_type=F32)


def head_cols(head):
    return slice(head * HEAD_DIM, (head + 1) * HEAD_DIM)


def staggered(items, scores_at, finish):
    scores = scores_at(items[0])
    for at, item in enumerate(items):
        later = scores_at(items[at + 1]) if at + 1 < len(items) else None
        finish(item, scores)
        scores = later


def question_kernel(
    place_ref,
    order_ref,
    query_ref,
    key_ref,
    value_ref,
    self_key_ref,
    self_value_ref,
    order_row_ref,
    out_ref,
    self_ref,
    self_lse_ref,
):
    lane = lax.broadcasted_iota(jnp.int32, (QROWS, EXTRA), 1)
    packed = [jnp.zeros((QROWS, EXTRA), F32)]
    first = pl.multiple_of((place_ref[2] // 2) * 16, 16)
    upper = place_ref[2] % 2 == 1
    row_ids = lax.broadcasted_iota(jnp.int32, (16, QROWS), 0)
    row_order = jnp.zeros((16, QROWS), jnp.int32)
    for row in range(16):
        row_order = jnp.where(row_ids == row, order_ref[first + row], row_order)
    allowed = jnp.concatenate([order_row_ref[...] <= row_order] * GROUP, axis=0)
    lse = jnp.zeros((8, EXTRA), F32)

    def scores_at(head):
        return scores_of(query_ref[:, head_cols(head)], key_ref[:, head_cols(head // GROUP)])

    def finish(head, scores):
        maxima, weights, totals = weigh(scores)
        summed = times_values(weights, value_ref[:, head_cols(head // GROUP)])
        out_ref[:, head_cols(head)] = (summed / totals).astype(BF16)
        packed[0] = jnp.where(lane == head, maxima * SCALE + jnp.log2(totals), packed[0])

    staggered(range(HEADS), scores_at, finish)
    rest, terms = packed[0], None
    for part in range(3):
        term = rest.astype(BF16).astype(F32)
        rest = rest - term
        terms = term if part == 0 else terms + pltpu.roll(term, part * HEADS, 1)
    out_ref[:, HEADS * HEAD_DIM :] = terms.astype(BF16)

    for kv in range(HEADS // GROUP):
        heads = range(kv * GROUP, (kv + 1) * GROUP)
        queries = jnp.concatenate(
            [query_ref[pl.ds(first, 16), head_cols(head)] for head in heads], axis=0
        )
        scores = scores_of(queries, self_key_ref[:, head_cols(kv)])
        maxima, weights, totals = weigh(jnp.where(allowed, scores, -jnp.inf))
        summed = times_values(weights, self_value_ref[:, head_cols(kv)]) / totals
        row_lse = maxima * SCALE + jnp.log2(totals)
        for at, head in enumerate(heads):
            low, high = slice(at * 16, at * 16 + 8), slice(at * 16 + 8, at * 16 + 16)
            self_ref[:, head_cols(head)] = jnp.where(upper, summed[high], summed[low])
            lse = jnp.where(lane[:8] == head, jnp.where(upper, row_lse[high], row_lse[low]), lse)
    self_lse_ref[...] = lse


def question_part(
    place, quest_query, ctx_key, ctx_value, quest_key, quest_value, quest_order
):
    rows, width = quest_query.shape
    return pl.pallas_call(
        question_kernel,
        out_shape=(
            jax.ShapeDtypeStruct((rows, width + EXTRA), BF16),
            jax.ShapeDtypeStruct((8, width), F32),
            jax.ShapeDtypeStruct((8, EXTRA), F32),
        ),
        grid=(1,),
        in_specs=[
            SCALARS,
            SCALARS,
            whole(rows, width),
            whole(*ctx_key.shape),
            whole(*ctx_value.shape),
            whole(*quest_key.shape),
            whole(*quest_value.shape),
            whole(1, QROWS),
        ],
        out_specs=(whole(rows, width + EXTRA), whole(8, width), whole(8, EXTRA)),
        compiler_params=pltpu.CompilerParams(vmem_limit_bytes=VMEM_LIMIT),
        cost_estimate=pl.CostEstimate(flops=1 << 26, bytes_accessed=1 << 18, transcendentals=1 << 16),
        name="question_block",
    )(
        place,
        quest_order,
        quest_query,
        ctx_key,
        ctx_value,
        quest_key,
        quest_value,
        quest_order.reshape(1, QROWS),
    )


def combine_kernel(
    parts_hbm, self_ref, self_lse_ref, weight_hbm, out_ref, parts_ref, weight_ref, sems
):
    step = out_ref.shape[2]
    arrived = pltpu.make_async_copy(parts_hbm, parts_ref, sems.at[4])
    arrived.start()
    loads = []
    for at in range(out_ref.shape[0]):
        cols = pl.ds(at * step, step)
        loads.append(
            pltpu.make_async_copy(weight_hbm.at[:, cols], weight_ref.at[:, cols], sems.at[at])
        )
        loads[-1].start()
    arrived.wait()
    blocks = parts_ref.shape[0] // 8
    width = HEADS * HEAD_DIM
    terms = parts_ref[:, width:].astype(F32)
    lse = terms + pltpu.roll(terms, EXTRA - HEADS, 1) + pltpu.roll(terms, EXTRA - 2 * HEADS, 1)
    lse = lse.reshape(blocks, 8, EXTRA)
    peak = jnp.maximum(jnp.max(lse, axis=0), self_lse_ref[...])
    scale = jnp.exp2(lse - peak[None])
    self_scale = jnp.exp2(self_lse_ref[...] - peak)
    inverse = 1.0 / (jnp.sum(scale, axis=0) + self_scale)
    scale = scale * inverse[None]
    self_scale = self_scale * inverse
    attended = []
    for head in range(HEADS):
        total = self_ref[:, head_cols(head)] * self_scale[:, head : head + 1]
        part = parts_ref[:, head_cols(head)].astype(F32).reshape(blocks, 8, HEAD_DIM)
        attended.append(total + jnp.sum(part * scale[:, :, head : head + 1], axis=0))
    attended = jnp.concatenate(attended, axis=1).astype(BF16)
    for at, load in enumerate(loads):
        load.wait()
        out_ref[at] = jnp.dot(
            attended, weight_ref[:, at * step : (at + 1) * step], preferred_element_type=F32
        )


def combine_part(parts, self_out, self_lse, out_weight):
    depth, columns = out_weight.shape
    return pl.pallas_call(
        combine_kernel,
        out_shape=jax.ShapeDtypeStruct((4, 8, columns // 4), F32),
        grid=(1,),
        in_specs=[
            pl.BlockSpec(memory_space=pltpu.HBM),
            whole(*self_out.shape),
            whole(*self_lse.shape),
            pl.BlockSpec(memory_space=pltpu.HBM),
        ],
        out_specs=whole(4, 8, columns // 4),
        scratch_shapes=[
            pltpu.VMEM(parts.shape, BF16),
            pltpu.VMEM((depth, columns), BF16),
            pltpu.SemaphoreType.DMA((5,)),
        ],
        compiler_params=pltpu.CompilerParams(vmem_limit_bytes=VMEM_LIMIT),
        cost_estimate=pl.CostEstimate(flops=2 * 8 * depth * columns, bytes_accessed=9 << 20, transcendentals=0),
        name="question_merge",
    )(parts, self_out, self_lse, out_weight)


def local_kernel(
    place_ref, query_ref, key_ref, value_ref, sum_out, stat_out, sum_ref, stat_ref, sems
):
    copies = []

    def send(source, target, rows):
        copy = pltpu.make_async_copy(source.at[rows], target.at[rows], sems.at[len(copies)])
        copy.start()
        copies.append(copy)

    row_ids = lax.broadcasted_iota(jnp.int32, (TILE, TILE), 0)
    col_ids = lax.broadcasted_iota(jnp.int32, (TILE, TILE), 1)
    causal = col_ids <= row_ids
    lane = lax.broadcasted_iota(jnp.int32, (TILE, EXTRA), 1)
    stats = {}

    def scores_at(item):
        tile, head = item
        rows = slice(tile * TILE, (tile + 1) * TILE)
        return scores_of(query_ref[rows, head_cols(head)], key_ref[: (tile + 1) * TILE, :])

    def finish(item, scores):
        tile, head = item
        rows = slice(tile * TILE, (tile + 1) * TILE)
        before = tile * TILE
        last = jnp.where(causal, scores[:, before:], -jnp.inf)
        scores = jnp.concatenate([scores[:, :before], last], axis=1) if before else last
        maxima, weights, totals = weigh(scores)
        values = value_ref[: before + TILE, :]
        sum_ref[rows, head_cols(head)] = times_values(weights, values)
        stat = stats.get(tile, jnp.zeros((TILE, EXTRA), F32))
        stat = jnp.where(lane == head, maxima, stat)
        stats[tile] = jnp.where(lane == GROUP + head, totals, stat)
        if head == GROUP - 1:
            stat_ref[rows, :] = stats[tile]
            send(sum_ref, sum_out, rows)
            send(stat_ref, stat_out, rows)

    tiles = range(BLOCK // TILE - 1, -1, -1)
    staggered([(tile, head) for tile in tiles for head in range(GROUP)], scores_at, finish)
    for copy in copies:
        copy.wait()


def local_part(turn, place, ctx_query, ctx_key, ctx_value):
    rows = ctx_query.shape[0]
    group = GROUP * HEAD_DIM
    at_head = lambda step, place: (0, place[turn])
    return pl.pallas_call(
        local_kernel,
        out_shape=(
            jax.ShapeDtypeStruct((rows, group), F32),
            jax.ShapeDtypeStruct((rows, EXTRA), F32),
        ),
        grid_spec=pltpu.PrefetchScalarGridSpec(
            num_scalar_prefetch=1,
            grid=(1,),
            in_specs=[
                pl.BlockSpec((rows, group), at_head),
                pl.BlockSpec((rows, HEAD_DIM), at_head),
                pl.BlockSpec((rows, HEAD_DIM), at_head),
            ],
            out_specs=(pl.BlockSpec(memory_space=pltpu.HBM),) * 2,
            scratch_shapes=[
                pltpu.VMEM((rows, group), F32),
                pltpu.VMEM((rows, EXTRA), F32),
                pltpu.SemaphoreType.DMA((2 * rows // TILE,)),
            ],
        ),
        compiler_params=pltpu.CompilerParams(vmem_limit_bytes=VMEM_LIMIT),
        cost_estimate=pl.CostEstimate(flops=1 << 26, bytes_accessed=1 << 18, transcendentals=1 << 16),
        name="context_own",
    )(place, ctx_query, ctx_key, ctx_value)


def anchor_kernel(place_ref, query_ref, *refs):
    out_ref, summed_ref = refs[-2:]
    is_anchor = place_ref[2] == 0
    lane = lax.broadcasted_iota(jnp.int32, (TILE, EXTRA), 1)

    def run(key_ref, value_ref, sum_ref, stat_ref):
        packed = {}

        def scores_at(item):
            row, head = item
            return scores_of(query_ref[row : row + TILE, head_cols(head)], key_ref[...])

        def finish(item, scores):
            row, head = item
            rows = slice(row, row + TILE)
            maxima, weights, totals = weigh(scores)
            summed_ref[rows, head_cols(head)] = times_values(weights, value_ref[...])
            all_maxima, all_totals = packed.get(row, (jnp.zeros((TILE, EXTRA), F32),) * 2)
            all_maxima = jnp.where(lane == head, maxima, all_maxima)
            all_totals = jnp.where(lane == head, totals, all_totals)
            packed[row] = all_maxima, all_totals
            if head == GROUP - 1:
                merge(rows, all_maxima, all_totals)

        def merge(rows, maxima, totals):
            own_max = stat_ref[rows, :]
            own_total = pltpu.roll(own_max, EXTRA - GROUP, 1)
            maxima = jnp.where(is_anchor, -jnp.inf, maxima)
            peak = jnp.maximum(maxima, own_max)
            scale = jnp.exp2((maxima - peak) * SCALE)
            own_scale = jnp.exp2((own_max - peak) * SCALE)
            inverse = 1.0 / (totals * scale + own_total * own_scale)
            scale, own_scale = scale * inverse, own_scale * inverse
            for head in range(GROUP):
                cols = head_cols(head)
                out_ref[rows, cols] = (
                    summed_ref[rows, cols] * scale[:, head : head + 1]
                    + sum_ref[rows, cols] * own_scale[:, head : head + 1]
                ).astype(BF16)

        rows = range(0, ANCHOR_ROWS, TILE)
        staggered([(row, head) for row in rows for head in range(GROUP)], scores_at, finish)

    @pl.when(pl.program_id(0) == 0)
    def _():
        run(*refs[:4])

    @pl.when(pl.program_id(0) == 1)
    def _():
        run(*refs[4:8])


def anchor_part(place, ctx_query, here, own_here, there, own_there):
    rows, width = ctx_query.shape
    group = GROUP * HEAD_DIM
    last = rows // ANCHOR_ROWS - 1
    tile_of = lambda turn, tile, place: (tile, place[turn])
    first_turn = lambda turn, tile, place: (jnp.where(turn == 0, tile, last), 0)
    second_turn = lambda turn, tile, place: (jnp.where(turn == 0, 0, tile), 0)
    keys = pl.BlockSpec((BLOCK, HEAD_DIM), lambda turn, tile, place: (0, 0))
    values = pl.BlockSpec((BLOCK, HEAD_DIM), lambda turn, tile, place: (0, 1))
    in_specs = [pl.BlockSpec((ANCHOR_ROWS, group), tile_of)]
    for row_of in (first_turn, second_turn):
        in_specs += [keys, values]
        in_specs += [pl.BlockSpec((ANCHOR_ROWS, columns), row_of) for columns in (group, EXTRA)]
    return pl.pallas_call(
        anchor_kernel,
        out_shape=jax.ShapeDtypeStruct((rows, width), BF16),
        grid_spec=pltpu.PrefetchScalarGridSpec(
            num_scalar_prefetch=1,
            grid=(2, rows // ANCHOR_ROWS),
            in_specs=in_specs,
            out_specs=pl.BlockSpec((ANCHOR_ROWS, group), tile_of),
            scratch_shapes=[pltpu.VMEM((ANCHOR_ROWS, group), F32)],
        ),
        compiler_params=pltpu.CompilerParams(vmem_limit_bytes=VMEM_LIMIT),
        cost_estimate=pl.CostEstimate(flops=1 << 31, bytes_accessed=1 << 20, transcendentals=1 << 16),
        name="context_anchor",
    )(place, ctx_query, here, here, *own_here, there, there, *own_there)


def after(value, *others):
    return lax.optimization_barrier((value, *others))[0]


def device_at(z, y, core):
    return (z * 4 + y) * 2 + core


def edges(phase, steps):
    pairs = []
    for core in range(2):
        for first, last in steps:
            for other in range(1 if phase == 0 else 4):
                along_y = (core == 0) == (phase == 0)
                ends = [
                    device_at(other, at, core) if along_y else device_at(at, other, core)
                    for at in (first, last)
                ]
                pairs.append(tuple(ends))
    return pairs


def exchange(value, axis):
    return lax.all_to_all(value, axis, split_axis=0, concat_axis=0, tiled=True)


def per_device(
    ctx_query, ctx_key, ctx_value, quest_query, quest_key, quest_value, quest_order, out_weight
):
    me = lax.axis_index("ctx").astype(jnp.int32)
    devices = lax.axis_size("ctx")
    core = lax.rem(me, 2)
    place = jnp.stack([core, 1 - core, me])
    siblings = [(at, at ^ 1) for at in range(devices)]

    def head_of(at):
        cols = slice(at * HEAD_DIM, (at + 1) * HEAD_DIM)
        return jnp.concatenate([ctx_key[:, cols], ctx_value[:, cols]], axis=1)

    def send(value, *steps):
        return lax.ppermute(value, "ctx", edges(*steps))

    moved = lax.ppermute(head_of(1), "ctx", [(0, 1)])
    half = jnp.where(me == 0, head_of(0), moved)
    moved = send(half, 0, [(0, 1)])
    parts, self_out, self_lse = question_part(
        place, quest_query, ctx_key, ctx_value, quest_key, quest_value, quest_order
    )
    half = half + after(moved, self_lse)
    moved = send(half, 0, [(0, 3), (1, 2)])
    width = parts.shape[1]
    parts = exchange(after(parts, half).reshape(devices, -1, width), "ctx").reshape(QROWS, width)
    own_here = local_part(0, place, after(ctx_query, half), ctx_key, ctx_value)
    half = half + after(moved, own_here[1])
    moved = send(half, 1, [(0, 1)])
    own_there = local_part(1, place, after(ctx_query, half), ctx_key, ctx_value)
    half = half + after(moved, own_there[1])
    moved = send(half, 1, [(0, 3), (1, 2)])
    projected = combine_part(after(parts, half), self_out, self_lse, out_weight)
    half = half + after(moved, projected)
    other_half = lax.ppermute(half, "ctx", siblings)
    projected = exchange(after(projected, half), "head")
    ctx_out = anchor_part(place, ctx_query, half, own_here, other_half, own_there)
    answer = jnp.sum(after(projected, ctx_out), axis=0).astype(BF16)
    return (ctx_out, answer)


def solution(mesh):
    in_specs = (
        P("ctx", "head"),
        P("ctx", "head"),
        P("ctx", "head"),
        P(None, "head"),
        P(None, "head"),
        P(None, "head"),
        P(),
        P("head", None),
    )
    out_specs = (P("ctx", "head"), P("ctx", "head"))
    return jax.shard_map(
        per_device, mesh=mesh, in_specs=in_specs, out_specs=out_specs, check_vma=False
    )
```

```python
import math

import jax
import jax.numpy as jnp
from jax import lax
from jax.experimental import pallas as pl
from jax.experimental.pallas import tpu as pltpu
from jax.sharding import PartitionSpec as P

HEAD_DIM = 128
BLOCK = 1024
TILE = 256
QROWS = 256
GROUP = 4
HEADS = 8
EXTRA = 128
SCALE = math.log2(math.e) / math.sqrt(HEAD_DIM)
F32 = jnp.float32
BF16 = jnp.bfloat16
VMEM_LIMIT = 56 * 1024 * 1024
ANCHOR_ROWS = 512


def scores_of(queries, keys):
    return lax.dot_general(queries, keys, (((1,), (1,)), ((), ())), preferred_element_type=F32)


def weigh(scores):
    maxima = jnp.max(scores, axis=-1, keepdims=True)
    weights = jnp.exp2((scores - maxima) * SCALE)
    return maxima, weights, jnp.sum(weights, axis=-1, keepdims=True)


def whole(*shape):
    return pl.BlockSpec(shape, lambda step: (0,) * len(shape))


def columns_of(rows, width, at):
    return pl.BlockSpec((rows, width), lambda step: (0, at))


SCALARS = pl.BlockSpec(memory_space=pltpu.SMEM)


def times_values(weights, values):
    return jnp.dot(weights.astype(BF16), values, preferred_element_type=F32)


def head_cols(head):
    return slice(head * HEAD_DIM, (head + 1) * HEAD_DIM)


def staggered(items, scores_at, finish):
    scores = scores_at(items[0])
    for at, item in enumerate(items):
        later = scores_at(items[at + 1]) if at + 1 < len(items) else None
        finish(item, scores)
        scores = later


def question_kernel(
    place_ref,
    order_ref,
    query_ref,
    key_ref,
    value_ref,
    self_key_ref,
    self_value_ref,
    order_row_ref,
    out_ref,
    self_ref,
    self_lse_ref,
):
    lane = lax.broadcasted_iota(jnp.int32, (QROWS, EXTRA), 1)
    packed = [jnp.zeros((QROWS, EXTRA), F32)]
    first = pl.multiple_of((place_ref[2] // 2) * 16, 16)
    upper = place_ref[2] % 2 == 1
    row_ids = lax.broadcasted_iota(jnp.int32, (16, QROWS), 0)
    row_order = jnp.zeros((16, QROWS), jnp.int32)
    for row in range(16):
        row_order = jnp.where(row_ids == row, order_ref[first + row], row_order)
    allowed = jnp.concatenate([order_row_ref[...] <= row_order] * GROUP, axis=0)
    lse = jnp.zeros((8, EXTRA), F32)

    def scores_at(head):
        return scores_of(query_ref[:, head_cols(head)], key_ref[:, head_cols(head // GROUP)])

    def finish(head, scores):
        maxima, weights, totals = weigh(scores)
        summed = times_values(weights, value_ref[:, head_cols(head // GROUP)])
        out_ref[:, head_cols(head)] = (summed / totals).astype(BF16)
        packed[0] = jnp.where(lane == head, maxima * SCALE + jnp.log2(totals), packed[0])

    staggered(range(HEADS), scores_at, finish)
    rest, terms = packed[0], None
    for part in range(3):
        term = rest.astype(BF16).astype(F32)
        rest = rest - term
        terms = term if part == 0 else terms + pltpu.roll(term, part * HEADS, 1)
    out_ref[:, HEADS * HEAD_DIM :] = terms.astype(BF16)

    for kv in range(HEADS // GROUP):
        heads = range(kv * GROUP, (kv + 1) * GROUP)
        queries = jnp.concatenate(
            [query_ref[pl.ds(first, 16), head_cols(head)] for head in heads], axis=0
        )
        scores = scores_of(queries, self_key_ref[:, head_cols(kv)])
        maxima, weights, totals = weigh(jnp.where(allowed, scores, -jnp.inf))
        summed = times_values(weights, self_value_ref[:, head_cols(kv)]) / totals
        row_lse = maxima * SCALE + jnp.log2(totals)
        for at, head in enumerate(heads):
            low, high = slice(at * 16, at * 16 + 8), slice(at * 16 + 8, at * 16 + 16)
            self_ref[:, head_cols(head)] = jnp.where(upper, summed[high], summed[low])
            lse = jnp.where(lane[:8] == head, jnp.where(upper, row_lse[high], row_lse[low]), lse)
    self_lse_ref[...] = lse


def question_part(
    place, quest_query, ctx_key, ctx_value, quest_key, quest_value, quest_order
):
    rows, width = quest_query.shape
    return pl.pallas_call(
        question_kernel,
        out_shape=(
            jax.ShapeDtypeStruct((rows, width + EXTRA), BF16),
            jax.ShapeDtypeStruct((8, width), F32),
            jax.ShapeDtypeStruct((8, EXTRA), F32),
        ),
        grid=(1,),
        in_specs=[
            SCALARS,
            SCALARS,
            whole(rows, width),
            whole(*ctx_key.shape),
            whole(*ctx_value.shape),
            whole(*quest_key.shape),
            whole(*quest_value.shape),
            whole(1, QROWS),
        ],
        out_specs=(whole(rows, width + EXTRA), whole(8, width), whole(8, EXTRA)),
        compiler_params=pltpu.CompilerParams(vmem_limit_bytes=VMEM_LIMIT),
        cost_estimate=pl.CostEstimate(flops=1 << 26, bytes_accessed=1 << 18, transcendentals=1 << 16),
        name="question_block",
    )(
        place,
        quest_order,
        quest_query,
        ctx_key,
        ctx_value,
        quest_key,
        quest_value,
        quest_order.reshape(1, QROWS),
    )


def combine_kernel(
    parts_hbm,
    self_hbm,
    self_lse_hbm,
    weight_hbm,
    out_ref,
    parts_ref,
    self_ref,
    self_lse_ref,
    weight_ref,
    sems,
):
    step = out_ref.shape[2]
    arrived = [
        pltpu.make_async_copy(parts_hbm, parts_ref, sems.at[4]),
        pltpu.make_async_copy(self_hbm, self_ref, sems.at[5]),
        pltpu.make_async_copy(self_lse_hbm, self_lse_ref, sems.at[6]),
    ]
    for copy in arrived:
        copy.start()
    loads = []
    for at in range(out_ref.shape[0]):
        cols = pl.ds(at * step, step)
        loads.append(
            pltpu.make_async_copy(weight_hbm.at[:, cols], weight_ref.at[:, cols], sems.at[at])
        )
        loads[-1].start()
    for copy in arrived:
        copy.wait()
    blocks = parts_ref.shape[0] // 8
    width = HEADS * HEAD_DIM
    terms = parts_ref[:, width:].astype(F32)
    lse = terms + pltpu.roll(terms, EXTRA - HEADS, 1) + pltpu.roll(terms, EXTRA - 2 * HEADS, 1)
    lse = lse.reshape(blocks, 8, EXTRA)
    peak = jnp.maximum(jnp.max(lse, axis=0), self_lse_ref[...])
    scale = jnp.exp2(lse - peak[None])
    self_scale = jnp.exp2(self_lse_ref[...] - peak)
    inverse = 1.0 / (jnp.sum(scale, axis=0) + self_scale)
    scale = scale * inverse[None]
    self_scale = self_scale * inverse
    attended = []
    for head in range(HEADS):
        total = self_ref[:, head_cols(head)] * self_scale[:, head : head + 1]
        part = parts_ref[:, head_cols(head)].astype(F32).reshape(blocks, 8, HEAD_DIM)
        attended.append(total + jnp.sum(part * scale[:, :, head : head + 1], axis=0))
    attended = jnp.concatenate(attended, axis=1).astype(BF16)
    for at, load in enumerate(loads):
        load.wait()
        out_ref[at] = jnp.dot(
            attended, weight_ref[:, at * step : (at + 1) * step], preferred_element_type=F32
        )


def combine_part(parts, self_out, self_lse, out_weight):
    depth, columns = out_weight.shape
    return pl.pallas_call(
        combine_kernel,
        out_shape=jax.ShapeDtypeStruct((4, 8, columns // 4), F32),
        grid=(1,),
        in_specs=[
            pl.BlockSpec(memory_space=pltpu.HBM),
            pl.BlockSpec(memory_space=pltpu.HBM),
            pl.BlockSpec(memory_space=pltpu.HBM),
            pl.BlockSpec(memory_space=pltpu.HBM),
        ],
        out_specs=whole(4, 8, columns // 4),
        scratch_shapes=[
            pltpu.VMEM(parts.shape, BF16),
            pltpu.VMEM(self_out.shape, F32),
            pltpu.VMEM(self_lse.shape, F32),
            pltpu.VMEM((depth, columns), BF16),
            pltpu.SemaphoreType.DMA((7,)),
        ],
        compiler_params=pltpu.CompilerParams(vmem_limit_bytes=VMEM_LIMIT),
        cost_estimate=pl.CostEstimate(flops=2 * 8 * depth * columns, bytes_accessed=9 << 20, transcendentals=0),
        name="question_merge",
    )(parts, self_out, self_lse, out_weight)


def local_kernel(
    place_ref, query_ref, key_ref, value_ref, sum_out, stat_out, sum_ref, stat_ref, sems
):
    copies = []

    def send(source, target, rows):
        copy = pltpu.make_async_copy(source.at[rows], target.at[rows], sems.at[len(copies)])
        copy.start()
        copies.append(copy)

    row_ids = lax.broadcasted_iota(jnp.int32, (TILE, TILE), 0)
    col_ids = lax.broadcasted_iota(jnp.int32, (TILE, TILE), 1)
    causal = col_ids <= row_ids
    lane = lax.broadcasted_iota(jnp.int32, (TILE, EXTRA), 1)
    stats = {}

    def scores_at(item):
        tile, head = item
        rows = slice(tile * TILE, (tile + 1) * TILE)
        return scores_of(query_ref[rows, head_cols(head)], key_ref[: (tile + 1) * TILE, :])

    def finish(item, scores):
        tile, head = item
        rows = slice(tile * TILE, (tile + 1) * TILE)
        before = tile * TILE
        last = jnp.where(causal, scores[:, before:], -jnp.inf)
        scores = jnp.concatenate([scores[:, :before], last], axis=1) if before else last
        maxima, weights, totals = weigh(scores)
        values = value_ref[: before + TILE, :]
        sum_ref[rows, head_cols(head)] = times_values(weights, values)
        stat = stats.get(tile, jnp.zeros((TILE, EXTRA), F32))
        stat = jnp.where(lane == head, maxima, stat)
        stats[tile] = jnp.where(lane == GROUP + head, totals, stat)
        if head == GROUP - 1:
            stat_ref[rows, :] = stats[tile]
            send(sum_ref, sum_out, rows)
            send(stat_ref, stat_out, rows)

    tiles = range(BLOCK // TILE - 1, -1, -1)
    staggered([(tile, head) for tile in tiles for head in range(GROUP)], scores_at, finish)
    for copy in copies:
        copy.wait()


def local_part(turn, place, ctx_query, ctx_key, ctx_value):
    rows = ctx_query.shape[0]
    group = GROUP * HEAD_DIM
    at_head = lambda step, place: (0, place[turn])
    return pl.pallas_call(
        local_kernel,
        out_shape=(
            jax.ShapeDtypeStruct((rows, group), F32),
            jax.ShapeDtypeStruct((rows, EXTRA), F32),
        ),
        grid_spec=pltpu.PrefetchScalarGridSpec(
            num_scalar_prefetch=1,
            grid=(1,),
            in_specs=[
                pl.BlockSpec((rows, group), at_head),
                pl.BlockSpec((rows, HEAD_DIM), at_head),
                pl.BlockSpec((rows, HEAD_DIM), at_head),
            ],
            out_specs=(pl.BlockSpec(memory_space=pltpu.HBM),) * 2,
            scratch_shapes=[
                pltpu.VMEM((rows, group), F32),
                pltpu.VMEM((rows, EXTRA), F32),
                pltpu.SemaphoreType.DMA((2 * rows // TILE,)),
            ],
        ),
        compiler_params=pltpu.CompilerParams(vmem_limit_bytes=VMEM_LIMIT),
        cost_estimate=pl.CostEstimate(flops=1 << 26, bytes_accessed=1 << 18, transcendentals=1 << 16),
        name="context_own",
    )(place, ctx_query, ctx_key, ctx_value)


def anchor_kernel(place_ref, query_ref, *refs):
    out_ref, summed_ref = refs[-2:]
    is_anchor = place_ref[2] == 0
    lane = lax.broadcasted_iota(jnp.int32, (TILE, EXTRA), 1)

    def run(key_ref, value_ref, sum_ref, stat_ref):
        packed = {}

        def scores_at(item):
            row, head = item
            return scores_of(query_ref[row : row + TILE, head_cols(head)], key_ref[...])

        def finish(item, scores):
            row, head = item
            rows = slice(row, row + TILE)
            maxima, weights, totals = weigh(scores)
            summed_ref[rows, head_cols(head)] = times_values(weights, value_ref[...])
            all_maxima, all_totals = packed.get(row, (jnp.zeros((TILE, EXTRA), F32),) * 2)
            all_maxima = jnp.where(lane == head, maxima, all_maxima)
            all_totals = jnp.where(lane == head, totals, all_totals)
            packed[row] = all_maxima, all_totals
            if head == GROUP - 1:
                merge(rows, all_maxima, all_totals)

        def merge(rows, maxima, totals):
            own_max = stat_ref[rows, :]
            own_total = pltpu.roll(own_max, EXTRA - GROUP, 1)
            maxima = jnp.where(is_anchor, -jnp.inf, maxima)
            peak = jnp.maximum(maxima, own_max)
            scale = jnp.exp2((maxima - peak) * SCALE)
            own_scale = jnp.exp2((own_max - peak) * SCALE)
            inverse = 1.0 / (totals * scale + own_total * own_scale)
            scale, own_scale = scale * inverse, own_scale * inverse
            for head in range(GROUP):
                cols = head_cols(head)
                out_ref[rows, cols] = (
                    summed_ref[rows, cols] * scale[:, head : head + 1]
                    + sum_ref[rows, cols] * own_scale[:, head : head + 1]
                ).astype(BF16)

        rows = range(0, ANCHOR_ROWS, TILE)
        staggered([(row, head) for row in rows for head in range(GROUP)], scores_at, finish)

    @pl.when(pl.program_id(0) == 0)
    def _():
        run(*refs[:4])

    @pl.when(pl.program_id(0) == 1)
    def _():
        run(*refs[4:8])


def anchor_part(place, ctx_query, here, own_here, there, own_there):
    rows, width = ctx_query.shape
    group = GROUP * HEAD_DIM
    last = rows // ANCHOR_ROWS - 1
    tile_of = lambda turn, tile, place: (tile, place[turn])
    first_turn = lambda turn, tile, place: (jnp.where(turn == 0, tile, last), 0)
    second_turn = lambda turn, tile, place: (jnp.where(turn == 0, 0, tile), 0)
    keys = pl.BlockSpec((BLOCK, HEAD_DIM), lambda turn, tile, place: (0, 0))
    values = pl.BlockSpec((BLOCK, HEAD_DIM), lambda turn, tile, place: (0, 1))
    in_specs = [pl.BlockSpec((ANCHOR_ROWS, group), tile_of)]
    for row_of in (first_turn, second_turn):
        in_specs += [keys, values]
        in_specs += [pl.BlockSpec((ANCHOR_ROWS, columns), row_of) for columns in (group, EXTRA)]
    return pl.pallas_call(
        anchor_kernel,
        out_shape=jax.ShapeDtypeStruct((rows, width), BF16),
        grid_spec=pltpu.PrefetchScalarGridSpec(
            num_scalar_prefetch=1,
            grid=(2, rows // ANCHOR_ROWS),
            in_specs=in_specs,
            out_specs=pl.BlockSpec((ANCHOR_ROWS, group), tile_of),
            scratch_shapes=[pltpu.VMEM((ANCHOR_ROWS, group), F32)],
        ),
        compiler_params=pltpu.CompilerParams(vmem_limit_bytes=VMEM_LIMIT),
        cost_estimate=pl.CostEstimate(flops=1 << 31, bytes_accessed=1 << 20, transcendentals=1 << 16),
        name="context_anchor",
    )(place, ctx_query, here, here, *own_here, there, there, *own_there)


def after(value, *others):
    return lax.optimization_barrier((value, *others))[0]


def device_at(z, y, core):
    return (z * 4 + y) * 2 + core


def edges(phase, steps):
    pairs = []
    for core in range(2):
        for first, last in steps:
            for other in range(1 if phase == 0 else 4):
                along_y = (core == 0) == (phase == 0)
                ends = [
                    device_at(other, at, core) if along_y else device_at(at, other, core)
                    for at in (first, last)
                ]
                pairs.append(tuple(ends))
    return pairs


def exchange(value, axis):
    return lax.all_to_all(value, axis, split_axis=0, concat_axis=0, tiled=True)


def per_device(
    ctx_query, ctx_key, ctx_value, quest_query, quest_key, quest_value, quest_order, out_weight
):
    me = lax.axis_index("ctx").astype(jnp.int32)
    devices = lax.axis_size("ctx")
    core = lax.rem(me, 2)
    place = jnp.stack([core, 1 - core, me])
    siblings = [(at, at ^ 1) for at in range(devices)]

    def head_of(at):
        cols = slice(at * HEAD_DIM, (at + 1) * HEAD_DIM)
        return jnp.concatenate([ctx_key[:, cols], ctx_value[:, cols]], axis=1)

    def send(value, *steps):
        return lax.ppermute(value, "ctx", edges(*steps))

    moved = lax.ppermute(head_of(1), "ctx", [(0, 1)])
    half = jnp.where(me == 0, head_of(0), moved)
    moved = send(half, 0, [(0, 1)])
    parts, self_out, self_lse = question_part(
        place, quest_query, ctx_key, ctx_value, quest_key, quest_value, quest_order
    )
    half = half + after(moved, self_lse)
    moved = send(half, 0, [(0, 3), (1, 2)])
    width = parts.shape[1]
    parts = exchange(after(parts, half).reshape(devices, -1, width), "ctx").reshape(QROWS, width)
    own_here = local_part(0, place, after(ctx_query, half), ctx_key, ctx_value)
    half = half + after(moved, own_here[1])
    moved = send(half, 1, [(0, 1)])
    own_there = local_part(1, place, after(ctx_query, half), ctx_key, ctx_value)
    half = half + after(moved, own_there[1])
    moved = send(half, 1, [(0, 3), (1, 2)])
    projected = combine_part(after(parts, half), self_out, self_lse, out_weight)
    half = half + after(moved, projected)
    other_half = lax.ppermute(half, "ctx", siblings)
    projected = exchange(after(projected, half), "head")
    ctx_out = anchor_part(place, ctx_query, half, own_here, other_half, own_there)
    answer = jnp.sum(after(projected, ctx_out), axis=0).astype(BF16)
    return (ctx_out, answer)


def solution(mesh):
    in_specs = (
        P("ctx", "head"),
        P("ctx", "head"),
        P("ctx", "head"),
        P(None, "head"),
        P(None, "head"),
        P(None, "head"),
        P(),
        P("head", None),
    )
    out_specs = (P("ctx", "head"), P("ctx", "head"))
    return jax.shard_map(
        per_device, mesh=mesh, in_specs=in_specs, out_specs=out_specs, check_vma=False
    )
```
